32 devices in a mesh: energy: 4 (over x, core), atom: 8 (over z, y).
Axes of the slice: x: 2, y: 2, z: 4, core: 2. Of those that a mesh axis runs over, the one named last changes fastest.
Arguments:
- green: bfloat16 [32, 2, 12, 12, 512], P('atom', None, None, None, 'energy'), may hold values from -6 to 6
- coupling: bfloat16 [32, 10368], P('atom'), may hold values from -0.375 to 0.375
- neighbours: int32 [32, 24], P('atom'), may hold values from 0 to 31, as said below
- shifts: int32 [16], replicated, may hold values from 1 to 64, as said below
- weights: float32 [16], replicated, may hold values from 0.1 to 1
Outputs:
- self_energy: bfloat16 [32, 2, 12, 12, 512], P('atom', None, None, None, 'energy')
The draws below stay inside these ranges and needn't reach their ends.
Inputs may be any that keep to these rules, and one draw needn't show every extreme that they name: `neighbours`: of the 24 x 4 entries in the rows of one device's atoms, exactly 12 name atoms held by other devices, at most 2 of them atoms of any one device, and in every draw some device's entries reach 2 for some other device; the other remote entries are spread evenly over the remaining devices. `shifts`: one of them equals 64.
All inputs are finite; a program needn't handle non-finite values.
Results may differ from the reference program's by a relative error of at most 0.012.
Values may be sent and summed in bfloat16 or wider, within the bound.
No kernel may reach another device: no remote copies, remote signals or barrier semaphores. Data moves between devices by JAX's collectives and lax.ppermute only.
A program may use at most 128 MiB of HBM per device.

```python
import math
import jax
import jax.numpy as jnp
from jax import lax

ORB = 12
NBR = 24
DIRS = 3
NQ = 16
MAXS = 64
CAP = 2
ATOM_DEV = 4
ATOMS = 32
NE = 512
REMOTE = 12
N_ATOM = 8


def draw_neighbours(key, part):
    slots = NBR * ATOM_DEV

    def one_device(device_key, device):
        key_perm, key_row, key_mix = jax.random.split(device_key, 3)
        others = (device + 1 + jax.random.permutation(key_perm, N_ATOM - 1)) % N_ATOM
        position = jnp.arange(slots)
        beyond = position - (slots - REMOTE) - CAP
        spread = others[1 + jnp.maximum(beyond, 0) % (N_ATOM - 2)]
        holder = jnp.where(position < slots - REMOTE, device, jnp.where(beyond < 0, others[0], spread))
        row_in = jax.random.randint(key_row, (slots,), 0, ATOM_DEV)
        atom_ids = holder * ATOM_DEV + row_in
        shuffle = jax.random.permutation(key_mix, slots)
        return atom_ids[shuffle].reshape(ATOM_DEV, NBR)
    device_keys = jax.random.split(jax.random.fold_in(key, 11), N_ATOM)
    drawn = jax.vmap(one_device)(device_keys, jnp.arange(N_ATOM))
    return drawn.reshape(ATOMS, NBR).astype(jnp.int32)


def draw_shifts(key, part):
    drawn = jax.random.randint(jax.random.fold_in(key, 23), (NQ,), 1, MAXS + 1)
    return drawn.at[0].set(MAXS).astype(jnp.int32)


def block_scale(own_key, extent, cuts, smallest, largest):
    loudness = 1.0
    for dim, shards_of in cuts:
        draws = jax.random.uniform(jax.random.fold_in(jax.random.fold_in(own_key, 6), dim), (shards_of,), jnp.float32, smallest / len(cuts), largest / len(cuts))
        loudness = loudness * jnp.repeat(jnp.exp(draws), extent[dim] // shards_of).reshape((-1,) + (1,) * (len(extent) - 1 - dim))
    return loudness


def normal_values(own_key, shape, scale, reach, shards=(), held_as=jnp.bfloat16):
    array = jax.random.normal(own_key, shape, jnp.float32) * scale
    if len(shards) > 0:
        array = block_scale(own_key, shape, shards, -0.22, 0.18) * array
    return jnp.clip(array, min=-reach, max=reach).astype(held_as)


def setup_inputs(seed: int = 0) -> dict:
    arg_keys = jax.random.split(jax.random.key(seed), 6)
    return {
        "green": normal_values(arg_keys[0], (ATOMS, 2, ORB, ORB, NE), 1.0, 6.0, ((0, 8), (4, 4))),
        "coupling": normal_values(arg_keys[1], (ATOMS, NBR * DIRS * ORB * ORB), (ORB * NBR) ** -0.5, 0.375, ((0, 8),)),
        "neighbours": draw_neighbours(jax.random.fold_in(arg_keys[5], 71), 0),
        "shifts": draw_shifts(jax.random.fold_in(arg_keys[5], 71), 0),
        "weights": jnp.clip(jnp.exp(jax.random.uniform(arg_keys[4], (NQ,), jnp.float32, math.log(0.1), math.log(1.0))), 0.1, 1.0),
    }


def convolve(blocks, shifts, weights, span_out):
    def add_term(term_index, running):
        window = lax.dynamic_slice_in_dim(blocks, shifts[term_index], span_out, blocks.ndim - 1)
        return running + weights[term_index] * window.astype(jnp.float32)
    zeroed = jnp.zeros(blocks.shape[:-1] + (span_out,), jnp.float32)
    return lax.fori_loop(0, shifts.shape[0], add_term, zeroed).astype(jnp.bfloat16)


def reference(green, coupling, neighbours, shifts, weights):
    atom_count = green.shape[0]
    energies = green.shape[-1]
    padded = jnp.concatenate([green, jnp.zeros(green.shape[:-1] + (MAXS,), green.dtype)], axis=4)
    convolved = convolve(padded, shifts, weights, energies)
    matrices = coupling.reshape(atom_count, NBR, DIRS, ORB, ORB)

    def one_atom(packed):
        matrix = packed[0].astype(jnp.float32)
        blocks = convolved[packed[1]].astype(jnp.float32)
        products = jnp.einsum("kdab,kpbce->kdpace", matrix, blocks).astype(jnp.bfloat16)
        summed = jnp.einsum("kdpace,kdfc->pafe", products.astype(jnp.float32), matrix)
        return summed.astype(jnp.bfloat16)

    return lax.map(one_atom, (matrices, neighbours))
```

```python
import jax
import jax.numpy as jnp
from jax import lax
from jax.experimental import pallas as pl
from jax.experimental.pallas import tpu as pltpu
from jax.sharding import PartitionSpec as P

MAXS = 64
CAP = 2
LANES = 128
PAD = 16
BF, F32, I32 = jnp.bfloat16, jnp.float32, jnp.int32
VM = pl.BlockSpec(memory_space=pltpu.VMEM)
SM = pl.BlockSpec(memory_space=pltpu.SMEM)
LIMIT = 40 * 2**20


def call(body, outs, ins, out_specs=None, scratch=(), flops=0, moved=0):
    return pl.pallas_call(
        body,
        out_shape=outs,
        in_specs=ins,
        out_specs=out_specs or [VM] * len(outs),
        scratch_shapes=list(scratch),
        compiler_params=pltpu.CompilerParams(vmem_limit_bytes=LIMIT),
        cost_estimate=pl.CostEstimate(flops=flops, bytes_accessed=moved, transcendentals=0),
    )


def dot(x, y):
    return jnp.dot(x, y, preferred_element_type=F32)


def iota(shape, dim):
    return lax.broadcasted_iota(I32, shape, dim)


def owner_row(entry, rows):
    if rows & (rows - 1) == 0:
        return lax.shift_right_logical(entry, rows.bit_length() - 1), lax.bitwise_and(entry, rows - 1)
    return lax.div(entry, rows), lax.rem(entry, rows)


def bands(shifts, weights, span):
    half = span // 2
    shape = (2 * span, span)
    lane = iota(shape, 1)
    gap = iota(shape, 0) - half - jnp.where(lane < half, lane, lane - half)
    band = jnp.zeros(shape, F32)
    for q in range(shifts.shape[0]):
        band = band + jnp.where(gap == shifts[q], weights[q], 0.0)
    high = band.astype(BF).astype(F32)
    return band, high, lane < half


def parted(part, first):
    zero = jnp.zeros_like(part)
    return jnp.concatenate([jnp.where(first, part, zero), jnp.where(first, zero, part)], axis=0).astype(BF)


def rows_apart(x, atoms):
    block = x.shape[0] // atoms
    size = block // 2
    to, of = iota((block, block), 0), iota((block, block), 1)
    pick = (of == jnp.where(to < size, 2 * to, 2 * (to - size) + 1)).astype(F32).astype(BF)
    wide = jnp.concatenate([x[a * block : (a + 1) * block] for a in range(atoms)], axis=1)
    return dot(pick, wide).astype(BF)


def beside(parts, atoms, span, size):
    stacked = []
    for a in range(atoms):
        stacked.append(
            jnp.concatenate(
                [y[p * size : (p + 1) * size, a * span : (a + 1) * span] for p in range(2) for y in parts], axis=1
            )
        )
    return jnp.concatenate(stacked, axis=0)


def low_kernel(shifts, weights, x, out):
    atoms, size, span = out.shape
    band, high, first = bands(shifts, weights, span)
    half = span // 2
    z = beside([rows_apart(x[...], atoms)], atoms, span, size)
    cut, first = slice(half, half + span), first[half : half + span]
    y = dot(z, parted(high[cut], first)) + dot(z, parted((band - high)[cut], first))
    out[...] = y.astype(BF).reshape(out.shape)


def high_kernel(shifts, weights, x, beyond, out):
    atoms, size, span = out.shape
    band, high, first = bands(shifts, weights, span)
    z = beside([rows_apart(x[...], atoms), rows_apart(beyond[...], atoms)], atoms, span, size)
    y = dot(z, parted(high, first)) + dot(z, parted(band - high, first))
    out[...] = y.astype(BF).reshape(out.shape)


def asked_by(names, holder, rows):
    def step(k, found):
        for a in range(names.shape[0]):
            owner, row = owner_row(names[a, k], rows)
            out = []
            for (count, picks), who in zip(found, holder):
                hit = owner == who
                picks = tuple(jnp.where(hit & (count == r), row, p) for r, p in enumerate(picks))
                out.append((count + hit.astype(I32), picks))
            found = tuple(out)
        return found

    zero = jnp.int32(0)
    start = tuple((zero, (zero,) * CAP) for _ in holder)
    return [picks for _, picks in lax.fori_loop(0, names.shape[1], step, start)]


def make_own(mates, half):
    def kernel(*refs):
        names, (low, high), outs, later = refs[:mates], refs[mates : mates + 2], refs[mates + 2 : -1], refs[-1]
        rows, _, span = low.shape
        me = lax.axis_index("atom")
        for s in range(mates):
            own, mirrored = asked_by(names[s], (me, lax.bitwise_xor(me, half)), rows)
            for r in range(CAP):
                outs[s][r, :, :span] = low[own[r]]
                outs[s][r, :, span:] = high[own[r]]
                later[s * CAP + r] = mirrored[r]

    return kernel


def make_relay(mates):
    def kernel(*refs):
        later, (low, high), outs = refs[0], refs[1:3], refs[3:]
        span = low.shape[2]
        for s in range(mates):
            for r in range(CAP):
                outs[s][r, :, :span] = low[later[s * CAP + r]]
                outs[s][r, :, span:] = high[later[s * CAP + r]]

    return kernel


def make_form(orb):
    size = orb * orb

    def kernel(names, x, ops_local, ops_far, place, left, right, local, count):
        atoms, nbr = names.shape
        terms = x.shape[0]
        dirs = terms // (atoms * nbr)
        me = lax.axis_index("atom")
        chunks = left.shape[0]
        wide = chunks * LANES
        source, lane = iota((size, wide), 0), iota((size, wide), 1)
        group = sum(((lane >= m * orb).astype(I32) for m in range(1, orb)), jnp.zeros((size, wide), I32))
        within = lane - group * orb
        real = lane < size
        values = x[...]
        zeros = jnp.zeros((terms, wide), F32)
        for i in range(PAD):
            if i < orb:
                spread = dot(values, ((source == i * orb + group) & real).astype(F32).astype(BF))
                filled = dot(values, ((source == i * orb + within) & real).astype(F32).astype(BF))
                for c in range(chunks):
                    left[c, i] = spread[:, c * LANES : (c + 1) * LANES]
            else:
                filled = zeros
            for c in range(chunks):
                right[c, pl.ds(i, terms, stride=PAD), :] = filled[:, c * LANES : (c + 1) * LANES]
        local[...] = jnp.zeros(local.shape, F32)
        for w in range(count.shape[0]):
            count[w] = 0
        for q in range(place.shape[0]):
            place[q] = -1

        def operator(base):
            for c in range(chunks):
                lanes = slice(c * LANES, (c + 1) * LANES)
                tiles = [right[c, pl.ds(pl.multiple_of((base + d) * PAD, PAD), PAD), :] for d in range(dirs)]
                for i in range(orb):
                    rows = [left[c, i, pl.ds(base + d, 1), :] * tiles[d] for d in range(dirs)]
                    yield slice(i * PAD, (i + 1) * PAD), lanes, sum(rows[1:], rows[0])

        def entry(k, carry):
            for a in range(atoms):
                base = (a * nbr + k) * dirs
                owner, row = owner_row(names[a, k], atoms)
                apart = lax.bitwise_xor(owner, me)

                @pl.when(apart == 0)
                def _():
                    for at, lanes, tile in operator(base):
                        local[a * atoms + row, at, lanes] += tile

                @pl.when(apart != 0)
                def _():
                    rank = count[owner]
                    count[owner] = rank + 1
                    slot = (apart - 1) * CAP + jnp.minimum(rank, CAP - 1)
                    place[slot] = a * atoms + row
                    for at, lanes, tile in operator(base):
                        ops_far[slot, at, lanes] = tile.astype(BF)

            return carry

        lax.fori_loop(0, nbr, entry, 0)
        ops_local[...] = local[...].astype(BF)

    return kernel


def make_final(mates, orb):
    size = orb * orb

    def kernel(*refs):
        place, ops_local, ops_far = refs[:3]
        own, mirror = refs[3:5], refs[5:7]
        near, far = refs[7 : 7 + mates], refs[7 + mates : 7 + 2 * mates]
        out, total = refs[-2:]
        atoms, tall, wide = total.shape
        span = wide // 2
        half = span // 2
        for a in range(atoms):
            run = jnp.zeros((tall, wide), F32)
            for b in range(atoms):
                run = run + dot(ops_local[a * atoms + b, :, :size], jnp.concatenate([own[0][b], own[1][b]], axis=1))
            total[a] = run

        def add(slot, block):
            spot = place[slot]

            @pl.when(spot >= 0)
            def _():
                to, row = owner_row(spot, atoms)
                total[to] += dot(ops_far[slot, :, :size], block(row))

        for s in range(mates):
            for r in range(CAP):
                add(s * CAP + r, lambda row: near[s][r])
        for r in range(CAP):
            add(mates * CAP + r, lambda row: jnp.concatenate([mirror[0][row], mirror[1][row]], axis=1))
        for s in range(mates):
            for r in range(CAP):
                add((mates + 1 + s) * CAP + r, lambda row: far[s][r])

        to, of = iota((2 * size, tall), 0), iota((2 * size, tall), 1)
        f = lax.bitwise_and(of, PAD - 1)
        at = 2 * (lax.shift_right_logical(of, PAD.bit_length() - 1) * orb + f)
        even = ((to == at) & (f < orb)).astype(F32).astype(BF)
        odd = ((to == at + 1) & (f < orb)).astype(F32).astype(BF)
        parts = [[], []]
        for a in range(atoms):
            for p in range(2):
                lanes = [total[a, :, h * span + p * half : h * span + (p + 1) * half] for h in range(2)]
                parts[p].append(jnp.concatenate(lanes, axis=1).astype(BF))
        rows = dot(even, jnp.concatenate(parts[0], axis=1)) + dot(odd, jnp.concatenate(parts[1], axis=1))
        for a in range(atoms):
            out[a * 2 * size : (a + 1) * 2 * size, :] = rows[:, a * span : (a + 1) * span].astype(BF)

    return kernel


def on_device(green, coupling, neighbours, shifts, weights):
    atoms, _, orb, _, span = green.shape
    size = orb * orb
    devices = lax.axis_size("atom")
    half = devices // 2
    mates = half - 1
    peers = lax.axis_size("energy")
    shape = jax.ShapeDtypeStruct

    def across(value, by):
        return lax.ppermute(value, "atom", [(i, i ^ by) for i in range(devices)])

    x = green.transpose(0, 2, 3, 1, 4).reshape(atoms * size * 2, span)
    beyond = lax.ppermute(x, "energy", [(i, i - 1) for i in range(1, peers)])
    unit = shape((atoms, size, span), BF)
    (low,) = call(low_kernel, [unit], [SM, SM, VM])(shifts, weights, x)
    (high,) = call(high_kernel, [unit], [SM, SM, VM, VM])(shifts, weights, x, beyond)
    mirror = across(low, half), across(high, half)
    names = [across(neighbours, s) for s in range(1, half)]

    pair = shape((CAP, size, 2 * span), BF)
    *own_out, later = call(
        make_own(mates, half),
        [pair] * mates + [shape((mates * CAP,), I32)],
        [SM] * mates + [VM] * 2,
        [VM] * mates + [SM],
    )(*names, low, high)
    near = [across(v, s + 1) for s, v in enumerate(own_out)]

    terms = coupling.reshape(-1, size)
    tall, wide = orb * PAD, pl.cdiv(size, LANES) * LANES
    far_slots = (devices - 1) * CAP
    ops_local, ops_far, place = call(
        make_form(orb),
        [shape((atoms * atoms, tall, wide), BF), shape((far_slots, tall, wide), BF), shape((far_slots,), I32)],
        [SM, VM],
        [VM, VM, SM],
        [
            pltpu.VMEM((wide // LANES, orb, terms.shape[0], LANES), F32),
            pltpu.VMEM((wide // LANES, terms.shape[0] * PAD, LANES), F32),
            pltpu.VMEM((atoms * atoms, tall, wide), F32),
            pltpu.SMEM((devices,), I32),
        ],
        flops=4 * 10**9,
        moved=8 * 10**6,
    )(neighbours, terms)

    relay_out = call(make_relay(mates), [pair] * mates, [SM, VM, VM])(later, *mirror)
    far = [across(v, s + 1) for s, v in enumerate(relay_out)]
    (out,) = call(
        make_final(mates, orb),
        [shape(x.shape, BF)],
        [SM] + [VM] * (6 + 2 * mates),
        None,
        [pltpu.VMEM((atoms, tall, 2 * span), F32)],
    )(place, ops_local, ops_far, low, high, *mirror, *near, *far)
    return out.reshape(atoms, orb, orb, 2, span).transpose(0, 3, 1, 2, 4)


def solution(mesh):
    placed = (P("atom", None, None, None, "energy"), P("atom", None), P("atom", None), P(), P())
    return jax.shard_map(
        on_device,
        mesh=mesh,
        in_specs=placed,
        out_specs=P("atom", None, None, None, "energy"),
        check_vma=False,
    )
```

```python
import jax
import jax.numpy as jnp
from jax import lax
from jax.experimental import pallas as pl
from jax.experimental.pallas import tpu as pltpu
from jax.sharding import PartitionSpec as P

CAP = 2
LANES = 128
PAD = 16
BF, F32, I32 = jnp.bfloat16, jnp.float32, jnp.int32
VM = pl.BlockSpec(memory_space=pltpu.VMEM)
SM = pl.BlockSpec(memory_space=pltpu.SMEM)


def call(body, outs, ins, out_specs=None, scratch=(), us=1.0, limit=40):
    return pl.pallas_call(
        body,
        out_shape=outs,
        in_specs=ins,
        out_specs=out_specs or [VM] * len(outs),
        scratch_shapes=list(scratch),
        compiler_params=pltpu.CompilerParams(vmem_limit_bytes=limit * 2**20),
        cost_estimate=pl.CostEstimate(flops=int(us * 10**9), bytes_accessed=1000, transcendentals=0),
    )


def dot(x, y):
    return jnp.dot(x, y, preferred_element_type=F32)


def iota(shape, dim):
    return lax.broadcasted_iota(I32, shape, dim)


def zero_one(mask):
    return mask.astype(F32).astype(BF)


def rows_apart(x, atoms):
    block = x.shape[0] // atoms
    size = block // 2
    to, of = iota((block, block), 0), iota((block, block), 1)
    pick = zero_one(of == jnp.where(to < size, 2 * to, 2 * (to - size) + 1))
    wide = jnp.concatenate([x[a * block : (a + 1) * block] for a in range(atoms)], axis=1)
    return dot(pick, wide).astype(BF)


def convolve_kernel(shifts, weights, x, beyond, out):
    atoms, size, wide = out.shape
    span = wide // 2
    gap = iota((2 * span, span), 0) - iota((2 * span, span), 1)
    band = jnp.zeros(gap.shape, F32)
    for q in range(shifts.shape[0]):
        band = band + jnp.where(gap == shifts[q], weights[q], 0.0)
    high = band.astype(BF)
    low = (band - high.astype(F32)).astype(BF)
    parts = rows_apart(x[...], atoms), rows_apart(beyond[...], atoms)
    for a in range(atoms):
        z = jnp.concatenate([y[:, a * span : (a + 1) * span] for y in parts], axis=1)
        y = (dot(z, high) + dot(z, low)).astype(BF)
        out[a] = jnp.concatenate([y[:size], y[size:]], axis=1)


def plan_kernel(names, table, target):
    atoms, nbr = names.shape
    devices = table.shape[0]
    me = lax.axis_index("atom")
    device = iota((devices, nbr), 0)
    ahead = zero_one(iota((nbr, nbr), 0) < iota((nbr, nbr), 1))
    lane = iota(table.shape, 1)
    found = jnp.zeros(table.shape, F32)
    seen = jnp.zeros((devices, 1), F32)
    for a in range(atoms):
        entry = names[a : a + 1, :]
        owner = lax.div(entry, atoms)
        row = entry - owner * atoms
        match = (jnp.broadcast_to(owner, (devices, nbr)) == device).astype(F32)
        rank = dot(match.astype(BF), ahead) + seen
        seen = seen + jnp.sum(match, axis=1, keepdims=True)
        rows = jnp.broadcast_to(row, (devices, nbr)).astype(F32)
        for r in range(CAP):
            here = jnp.where(rank == r, match, 0.0)
            found = found + jnp.where(lane == r, jnp.sum(here * rows, axis=1, keepdims=True), 0.0)
            if a:
                found = found + jnp.where(lane == CAP + r, a * jnp.sum(here, axis=1, keepdims=True), 0.0)
        own_rank = jnp.minimum(jnp.sum(match * rank, axis=0, keepdims=True), CAP - 1.0).astype(I32)
        target[a : a + 1, :] = jnp.where(owner == me, row * atoms + a, atoms * atoms + owner * CAP + own_rank)
    table[...] = found.astype(I32)


def make_fetch(mates, over):
    def kernel(*refs):
        tables, unit, outs = refs[:mates], refs[mates], refs[-mates:]
        holder = lax.bitwise_xor(lax.axis_index("atom"), over)
        for table, out in zip(tables, outs):
            for r in range(CAP):
                out[r] = unit[table[holder, r]]

    return kernel


def make_form(orb):
    size = orb * orb
    tail = size - LANES
    reps = LANES // tail
    groups = pl.cdiv(orb, reps)
    height = (orb + groups) * PAD

    def kernel(target, x, ops, left, right, sums):
        atoms, nbr = target.shape
        terms = x.shape[0]
        slots = ops.shape[0]
        dirs = terms // (atoms * nbr)
        source, lane = iota((size, LANES), 0), iota((size, LANES), 1)

        def spread(at):
            group = sum(((at >= m * orb).astype(I32) for m in range(1, orb)), jnp.zeros(at.shape, I32))
            return group, at - group * orb

        group, within = spread(lane)
        tail_group, tail_within = spread(LANES + lax.bitwise_and(lane, tail - 1))
        part = lax.shift_right_logical(lane, tail.bit_length() - 1)
        values = x[...]
        left_at, tail_at = source - group, source - part * orb - tail_group
        for i in range(orb):
            left[i] = dot(values, zero_one(left_at == i * orb)).astype(BF)
        for g in range(groups):
            left[orb + g] = dot(values, zero_one(tail_at == g * reps * orb)).astype(BF)
        right_at, tail_right = source - within, source - tail_within
        for f in range(orb):
            right[0, f] = dot(values, zero_one(right_at == f * orb)).astype(BF)
            right[1, f] = dot(values, zero_one(tail_right == f * orb)).astype(BF)
        behind = iota((nbr, terms), 1) - iota((nbr, terms), 0) * dirs
        mask = jnp.zeros((slots, terms), F32)
        for a in range(atoms):
            hit = zero_one(jnp.broadcast_to(target[a : a + 1, :], (slots, nbr)) == iota((slots, nbr), 0))
            shifted = behind - a * nbr * dirs
            mask = mask + dot(hit, zero_one((shifted >= 0) & (shifted < dirs)))
        mask = mask.astype(BF)
        for i in range(orb + groups):
            c = i // orb
            lhs = left[i]
            for f in range(0, orb, 2):
                pair = [lhs * right[c, f + m] for m in range(2)]
                found = dot(mask, jnp.concatenate(pair, axis=1))
                for m in range(2):
                    sums[pl.ds(i * PAD + f + m, slots, stride=height), :] = found[:, m * LANES : (m + 1) * LANES]
        at = lax.shift_right_logical(iota((PAD, LANES), 1), tail.bit_length() - 1)
        real = iota((PAD, LANES), 0) < orb

        def settle(slot, carry):
            base = slot * height

            def tile(i):
                return jnp.where(real, sums[pl.ds(pl.multiple_of(base + i * PAD, PAD), PAD), :], 0.0)

            packed = [tile(orb + g) for g in range(groups)]
            for i in range(orb):
                ops[slot, i * PAD : (i + 1) * PAD, :LANES] = tile(i).astype(BF)
                ops[slot, i * PAD : (i + 1) * PAD, LANES:] = jnp.where(at == i % reps, packed[i // reps], 0.0).astype(BF)
            return carry

        lax.fori_loop(0, slots, settle, 0, unroll=2)

    return kernel


def tall(block):
    tail = block.shape[0] - LANES
    return jnp.concatenate([block[:LANES]] + [block[LANES:]] * (LANES // tail), axis=0)


def make_local(mates, half):
    def kernel(*refs):
        table, ops = refs[:2]
        own, mirror = refs[2:4]
        near, total = refs[4 : 4 + mates], refs[-1]
        atoms, height, wide = total.shape
        me = lax.axis_index("atom")
        run = jnp.zeros((atoms * height, wide), F32)
        for b in range(atoms):
            block = tall(own[b])
            lhs = ops[b * atoms : (b + 1) * atoms].reshape(atoms * height, ops.shape[2])
            run = run + dot(lhs, block)
        total[...] = run.reshape(total.shape)
        for s in range(mates):
            for r in range(CAP):
                owner = lax.bitwise_xor(me, s + 1)
                total[table[owner, CAP + r]] += dot(ops[atoms * atoms + owner * CAP + r], tall(near[s][r]))
        for r in range(CAP):
            owner = lax.bitwise_xor(me, half)
            block = tall(mirror[table[owner, r]])
            total[table[owner, CAP + r]] += dot(ops[atoms * atoms + owner * CAP + r], block)

    return kernel


def make_final(mates, half, orb):
    size = orb * orb

    def kernel(*refs):
        table, ops, begun = refs[:3]
        far, out, total = refs[3 : 3 + mates], refs[-2], refs[-1]
        atoms, height, wide = total.shape
        span = wide // 2
        me = lax.axis_index("atom")
        total[...] = begun[...]
        for s in range(mates):
            for r in range(CAP):
                owner = lax.bitwise_xor(me, half + s + 1)
                total[table[owner, CAP + r]] += dot(ops[atoms * atoms + owner * CAP + r], tall(far[s][r]))

        to, of = iota((2 * size, height), 0), iota((2 * size, height), 1)
        f = lax.bitwise_and(of, PAD - 1)
        at = 2 * (lax.shift_right_logical(of, PAD.bit_length() - 1) * orb + f)
        even = zero_one((to == at) & (f < orb))
        odd = zero_one((to == at + 1) & (f < orb))
        parts = [[total[a, :, p * span : (p + 1) * span].astype(BF) for a in range(atoms)] for p in range(2)]
        rows = dot(even, jnp.concatenate(parts[0], axis=1)) + dot(odd, jnp.concatenate(parts[1], axis=1))
        for a in range(atoms):
            out[a * 2 * size : (a + 1) * 2 * size, :] = rows[:, a * span : (a + 1) * span].astype(BF)

    return kernel


def on_device(green, coupling, neighbours, shifts, weights):
    atoms, _, orb, _, span = green.shape
    size = orb * orb
    devices = lax.axis_size("atom")
    half = devices // 2
    mates = half - 1
    peers = lax.axis_size("energy")
    shape = jax.ShapeDtypeStruct

    def across(value, by):
        return lax.ppermute(value, "atom", [(i, i ^ by) for i in range(devices)])

    x = green.transpose(0, 2, 3, 1, 4).reshape(atoms * size * 2, span)
    beyond = lax.ppermute(x, "energy", [(i, i - 1) for i in range(1, peers)])
    table, target = call(
        plan_kernel, [shape((devices, LANES), I32), shape(neighbours.shape, I32)], [VM], us=3.0
    )(neighbours)
    tables = [across(table, s) for s in range(1, half)]
    (unit,) = call(convolve_kernel, [shape((atoms, size, 2 * span), BF)], [SM, SM, VM, VM], us=1.5)(
        shifts, weights, x, beyond
    )
    mirror = across(unit, half)
    pair = shape((CAP, size, 2 * span), BF)
    own_out = call(make_fetch(mates, 0), [pair] * mates, [SM] * mates + [VM])(*tables, unit)
    near = [across(v, s + 1) for s, v in enumerate(own_out)]

    terms = coupling.reshape(-1, size)
    height, groups = orb * PAD, pl.cdiv(orb, LANES // (size - LANES))
    slots = atoms * atoms + devices * CAP
    (ops,) = call(
        make_form(orb),
        [shape((slots, height, 2 * LANES), BF)],
        [VM, VM],
        None,
        [
            pltpu.VMEM((orb + groups, terms.shape[0], LANES), BF),
            pltpu.VMEM((2, orb, terms.shape[0], LANES), BF),
            pltpu.VMEM((slots * (height + groups * PAD), LANES), F32),
        ],
        us=5.0,
    )(target, terms)

    relay_out = call(
        make_fetch(mates, half), [pair] * mates, [SM] * mates + [VM, pl.BlockSpec(memory_space=pl.ANY)]
    )(*tables, mirror, ops)
    far = [across(v, s + 1) for s, v in enumerate(relay_out)]
    total = shape((atoms, height, 2 * span), F32)
    (begun,) = call(make_local(mates, half), [total], [SM] + [VM] * (3 + mates), us=2.0)(
        table, ops, unit, mirror, *near
    )
    (out,) = call(
        make_final(mates, half, orb),
        [shape(x.shape, BF)],
        [SM] + [VM] * (2 + mates),
        None,
        [pltpu.VMEM(total.shape, F32)],
    )(table, ops, begun, *far)
    return out.reshape(atoms, orb, orb, 2, span).transpose(0, 3, 1, 2, 4)


def solution(mesh):
    placed = (P("atom", None, None, None, "energy"), P("atom", None), P("atom", None), P(), P())
    return jax.shard_map(
        on_device,
        mesh=mesh,
        in_specs=placed,
        out_specs=P("atom", None, None, None, "energy"),
        check_vma=False,
    )
```

```python
import jax
import jax.numpy as jnp
from jax import lax
from jax.experimental import pallas as pl
from jax.experimental.pallas import tpu as pltpu
from jax.sharding import PartitionSpec as P

CAP = 2
LANES = 128
PAD = 16
SKEW = 8
BF, F32, I32 = jnp.bfloat16, jnp.float32, jnp.int32
VM = pl.BlockSpec(memory_space=pltpu.VMEM)
SM = pl.BlockSpec(memory_space=pltpu.SMEM)


def call(body, outs, ins, out_specs=None, scratch=(), us=1.0, limit=40):
    return pl.pallas_call(
        body,
        out_shape=outs,
        in_specs=ins,
        out_specs=out_specs or [VM] * len(outs),
        scratch_shapes=list(scratch),
        compiler_params=pltpu.CompilerParams(vmem_limit_bytes=limit * 2**20),
        cost_estimate=pl.CostEstimate(flops=int(us * 10**9), bytes_accessed=1000, transcendentals=0),
    )


def dot(x, y):
    return jnp.dot(x, y, preferred_element_type=F32)


def iota(shape, dim):
    return lax.broadcasted_iota(I32, shape, dim)


def zero_one(mask):
    return mask.astype(F32).astype(BF)


def rows_apart(x, atoms):
    block = x.shape[0] // atoms
    size = block // 2
    to, of = iota((block, block), 0), iota((block, block), 1)
    pick = zero_one(of == jnp.where(to < size, 2 * to, 2 * (to - size) + 1))
    wide = jnp.concatenate([x[a * block : (a + 1) * block] for a in range(atoms)], axis=1)
    return dot(pick, wide).astype(BF)


def beside(parts, atoms, span, size):
    rows = []
    for a in range(atoms):
        lanes = [y[p * size : (p + 1) * size, a * span : (a + 1) * span] for p in range(2) for y in parts]
        rows.append(jnp.concatenate(lanes, axis=1))
    return jnp.concatenate(rows, axis=0)


def low_kernel(spectrum, x, out, apart, bands):
    atoms, size, span = out.shape
    half = span // 2
    lane = iota((2 * span, span), 1)
    first = lane < half
    gap = (iota((2 * span, span), 0) - half - jnp.where(first, lane, lane - half)).astype(F32)
    band = jnp.zeros(gap.shape, F32)
    for q in range(spectrum.shape[1]):
        band = band + jnp.where(gap == spectrum[0, q], spectrum[1, q], 0.0)
    rounded = band.astype(BF).astype(F32)

    def parted(part, mask):
        return jnp.concatenate([jnp.where(mask, part, 0.0), jnp.where(mask, 0.0, part)], axis=0).astype(BF)

    bands[0] = parted(rounded, first)
    bands[1] = parted(band - rounded, first)
    y = rows_apart(x[...], atoms)
    apart[...] = y
    z = beside([y], atoms, span, size)
    cut = slice(half, half + span)
    y = dot(z, parted(rounded[cut], first[cut])) + dot(z, parted((band - rounded)[cut], first[cut]))
    out[...] = y.astype(BF).reshape(out.shape)


def high_kernel(apart, bands, beyond, out):
    atoms, size, span = out.shape
    z = beside([apart[...], rows_apart(beyond[...], atoms)], atoms, span, size)
    y = dot(z, bands[0]) + dot(z, bands[1])
    out[...] = y.astype(BF).reshape(out.shape)


def plan_kernel(names, table, target):
    atoms, nbr = names.shape
    devices = table.shape[0]
    me = lax.axis_index("atom")
    device = iota((devices, nbr), 0)
    ahead = zero_one(iota((nbr, nbr), 0) < iota((nbr, nbr), 1))
    lane = iota(table.shape, 1)
    found = jnp.zeros(table.shape, F32)
    seen = jnp.zeros((devices, 1), F32)
    for a in range(atoms):
        entry = names[a : a + 1, :]
        owner = lax.div(entry, atoms)
        row = entry - owner * atoms
        match = (jnp.broadcast_to(owner, (devices, nbr)) == device).astype(F32)
        rank = dot(match.astype(BF), ahead) + seen
        seen = seen + jnp.sum(match, axis=1, keepdims=True)
        rows = jnp.broadcast_to(row, (devices, nbr)).astype(F32)
        for r in range(CAP):
            here = jnp.where(rank == r, match, 0.0)
            found = found + jnp.where(lane == r, jnp.sum(here * rows, axis=1, keepdims=True), 0.0)
            if a:
                found = found + jnp.where(lane == CAP + r, a * jnp.sum(here, axis=1, keepdims=True), 0.0)
        own_rank = jnp.minimum(jnp.sum(match * rank, axis=0, keepdims=True), CAP - 1.0).astype(I32)
        target[a : a + 1, :] = jnp.where(owner == me, row * atoms + a, atoms * atoms + owner * CAP + own_rank)
    table[...] = found.astype(I32)


def make_first(mates, half):
    def kernel(*refs):
        tables, (low, high, mirror), outs = refs[:mates], refs[mates : mates + 3], refs[mates + 3 :]
        span = low.shape[2]
        me = lax.axis_index("atom")
        for table, out in zip(tables, outs):
            for r in range(CAP):
                row = table[me, r]
                out[r, :, :span] = low[row]
                out[r, :, span : 2 * span] = high[row]
                out[r, :, 2 * span :] = mirror[table[lax.bitwise_xor(me, half), r]]

    return kernel


def make_second(mates, half):
    def kernel(*refs):
        tables, mirror, outs = refs[:mates], refs[mates], refs[mates + 1 :]
        holder = lax.bitwise_xor(lax.axis_index("atom"), half)
        for table, out in zip(tables, outs):
            for r in range(CAP):
                out[r] = mirror[table[holder, r]]

    return kernel


def make_form(orb):
    size = orb * orb
    tail = size - LANES
    reps = LANES // tail
    groups = pl.cdiv(orb, reps)
    height = (orb + groups) * PAD + SKEW

    def kernel(target, x, ops, left, right, sums):
        atoms, nbr = target.shape
        terms = x.shape[0]
        slots = ops.shape[0]
        dirs = terms // (atoms * nbr)
        source, lane = iota((size, LANES), 0), iota((size, LANES), 1)

        def spread(at):
            group = sum(((at >= m * orb).astype(I32) for m in range(1, orb)), jnp.zeros(at.shape, I32))
            return group, at - group * orb

        group, within = spread(lane)
        tail_group, tail_within = spread(LANES + lax.bitwise_and(lane, tail - 1))
        part = lax.shift_right_logical(lane, tail.bit_length() - 1)
        values = x[...]
        left_at, tail_at = source - group, source - part * orb - tail_group
        for i in range(orb):
            left[i] = dot(values, zero_one(left_at == i * orb)).astype(BF)
        for g in range(groups):
            left[orb + g] = dot(values, zero_one(tail_at == g * reps * orb)).astype(BF)
        right_at, tail_right = source - within, source - tail_within
        for f in range(orb):
            right[0, f] = dot(values, zero_one(right_at == f * orb)).astype(BF)
            right[1, f] = dot(values, zero_one(tail_right == f * orb)).astype(BF)
        behind = iota((nbr, terms), 1) - iota((nbr, terms), 0) * dirs
        mask = jnp.zeros((slots, terms), F32)
        for a in range(atoms):
            hit = zero_one(jnp.broadcast_to(target[a : a + 1, :], (slots, nbr)) == iota((slots, nbr), 0))
            shifted = behind - a * nbr * dirs
            mask = mask + dot(hit, zero_one((shifted >= 0) & (shifted < dirs)))
        mask = mask.astype(BF)
        for i in range(orb + groups):
            c = i // orb
            lhs = left[i]
            for f in range(0, orb, 2):
                pair = [lhs * right[c, f + m] for m in range(2)]
                found = dot(mask, jnp.concatenate(pair, axis=1))
                for m in range(2):
                    sums[pl.ds(i * PAD + f + m, slots, stride=height), :] = found[:, m * LANES : (m + 1) * LANES]
        at = lax.shift_right_logical(iota((PAD, LANES), 1), tail.bit_length() - 1)
        only = [zero_one(at == m) for m in range(reps)]

        def settle(slot, carry):
            base = slot * height

            def tile(i):
                return sums[pl.ds(pl.multiple_of(base + i * PAD, PAD), PAD), :].astype(BF)

            packed = [tile(orb + g) for g in range(groups)]
            for i in range(orb):
                ops[slot, i * PAD : (i + 1) * PAD, :LANES] = tile(i)
                ops[slot, i * PAD : (i + 1) * PAD, LANES:] = packed[i // reps] * only[i % reps]
            return carry

        lax.fori_loop(0, slots, settle, 0, unroll=4)

    return kernel


def tall(block):
    tail = block.shape[0] - LANES
    return jnp.concatenate([block[:LANES]] + [block[LANES:]] * (LANES // tail), axis=0)


def make_local(mates, half):
    def kernel(*refs):
        table, ops = refs[:2]
        own, mirror = refs[2:4], refs[4:6]
        near, total = refs[6 : 6 + mates], refs[-1]
        atoms, height, wide = total.shape
        me = lax.axis_index("atom")
        run = jnp.zeros((atoms * height, wide), F32)
        for b in range(atoms):
            block = tall(jnp.concatenate([own[0][b], own[1][b]], axis=1))
            lhs = ops[b * atoms : (b + 1) * atoms].reshape(atoms * height, ops.shape[2])
            run = run + dot(lhs, block)
        total[...] = run.reshape(total.shape)
        for s in range(mates):
            for r in range(CAP):
                owner = lax.bitwise_xor(me, mates - s)
                total[table[owner, CAP + r]] += dot(ops[atoms * atoms + owner * CAP + r], tall(near[s][r, :, :wide]))
        for r in range(CAP):
            owner = lax.bitwise_xor(me, half)
            row = table[owner, r]
            block = tall(jnp.concatenate([mirror[0][row], mirror[1][row]], axis=1))
            total[table[owner, CAP + r]] += dot(ops[atoms * atoms + owner * CAP + r], block)

    return kernel


def make_final(mates, half, orb):
    size = orb * orb

    def kernel(*refs):
        table, ops, begun = refs[:3]
        first, second = refs[3 : 3 + mates], refs[3 + mates : 3 + 2 * mates]
        out, total = refs[-2:]
        atoms, height, wide = total.shape
        span = wide // 2
        part = span // 2
        me = lax.axis_index("atom")
        total[...] = begun[...]
        for s in range(mates):
            for r in range(CAP):
                owner = lax.bitwise_xor(me, half + mates - s)
                block = tall(jnp.concatenate([first[s][r, :, wide:], second[s][r]], axis=1))
                total[table[owner, CAP + r]] += dot(ops[atoms * atoms + owner * CAP + r], block)

        to, of = iota((2 * size, height), 0), iota((2 * size, height), 1)
        f = lax.bitwise_and(of, PAD - 1)
        at = 2 * (lax.shift_right_logical(of, PAD.bit_length() - 1) * orb + f)
        even = zero_one((to == at) & (f < orb))
        odd = zero_one((to == at + 1) & (f < orb))
        real = lax.bitwise_and(iota((height, span), 0), PAD - 1) < orb
        parts = [[], []]
        for a in range(atoms):
            for p in range(2):
                lanes = [total[a, :, h * span + p * part : h * span + (p + 1) * part] for h in range(2)]
                parts[p].append(jnp.where(real, jnp.concatenate(lanes, axis=1), 0.0).astype(BF))
        rows = dot(even, jnp.concatenate(parts[0], axis=1)) + dot(odd, jnp.concatenate(parts[1], axis=1))
        for a in range(atoms):
            out[a * 2 * size : (a + 1) * 2 * size, :] = rows[:, a * span : (a + 1) * span].astype(BF)

    return kernel


def after(value, *earlier):
    return lax.optimization_barrier((value,) + earlier)[0]


def on_device(green, coupling, neighbours, shifts, weights):
    atoms, _, orb, _, span = green.shape
    size = orb * orb
    devices = lax.axis_size("atom")
    half = devices // 2
    mates = half - 1
    peers = lax.axis_size("energy")
    shape = jax.ShapeDtypeStruct

    def across(value, by):
        return lax.ppermute(value, "atom", [(i, i ^ by) for i in range(devices)])

    x = green.transpose(0, 2, 3, 1, 4).reshape(atoms * size * 2, span)
    spectrum = jnp.stack([shifts.astype(F32), weights])
    unit = shape((atoms, size, span), BF)
    low, apart, bands = call(
        low_kernel,
        [unit, shape((2 * size, atoms * span), BF), shape((2, 4 * span, span), BF)],
        [SM, VM],
        us=1.2,
    )(spectrum, x)
    beyond = lax.ppermute(after(x, low), "energy", [(i, i - 1) for i in range(1, peers)])
    (high,) = call(high_kernel, [unit], [VM] * 3, us=0.7)(apart, bands, beyond)
    mirror = across(low, half), across(high, half)
    table, target = call(plan_kernel, [shape((devices, LANES), I32), shape(neighbours.shape, I32)], [VM], us=0.5)(
        neighbours
    )
    tables = [across(after(table, high), s) for s in reversed(range(1, half))]
    triple, single = shape((CAP, size, 3 * span), BF), shape((CAP, size, span), BF)
    first_out = call(make_first(mates, half), [triple] * mates, [SM] * mates + [VM] * 3)(*tables, low, high, mirror[0])
    near = [across(v, mates - s) for s, v in enumerate(first_out)]
    second_out = call(make_second(mates, half), [single] * mates, [SM] * mates + [VM])(*tables, mirror[1])
    far = [across(v, mates - s) for s, v in enumerate(second_out)]

    terms = coupling.reshape(-1, size)
    height, groups = orb * PAD, pl.cdiv(orb, LANES // (size - LANES))
    slots = atoms * atoms + devices * CAP
    (ops,) = call(
        make_form(orb),
        [shape((slots, height, 2 * LANES), BF)],
        [VM, VM],
        None,
        [
            pltpu.VMEM((orb + groups, terms.shape[0], LANES), BF),
            pltpu.VMEM((2, orb, terms.shape[0], LANES), BF),
            pltpu.VMEM(((slots + 1) * (height + groups * PAD + SKEW), LANES), F32),
        ],
        us=0.01,
    )(target, terms)

    total = shape((atoms, height, 2 * span), F32)
    (begun,) = call(make_local(mates, half), [total], [SM] + [VM] * (5 + mates), us=1.5)(
        table, ops, low, high, *mirror, *near
    )
    (out,) = call(
        make_final(mates, half, orb),
        [shape(x.shape, BF)],
        [SM] + [VM] * (2 + 2 * mates),
        None,
        [pltpu.VMEM(total.shape, F32)],
    )(table, ops, begun, *near, *far)
    return out.reshape(atoms, orb, orb, 2, span).transpose(0, 3, 1, 2, 4)


def solution(mesh):
    placed = (P("atom", None, None, None, "energy"), P("atom", None), P("atom", None), P(), P())
    return jax.shard_map(
        on_device,
        mesh=mesh,
        in_specs=placed,
        out_specs=P("atom", None, None, None, "energy"),
        check_vma=False,
    )
```

```python
import jax
import jax.numpy as jnp
from jax import lax
from jax.experimental import pallas as pl
from jax.experimental.pallas import tpu as pltpu
from jax.sharding import PartitionSpec as P

CAP = 2
LANES = 128
PAD = 16
SKEW = 8
BF, F32, I32 = jnp.bfloat16, jnp.float32, jnp.int32
VM = pl.BlockSpec(memory_space=pltpu.VMEM)
SM = pl.BlockSpec(memory_space=pltpu.SMEM)


def call(body, outs, ins, out_specs=None, scratch=(), us=1.0, limit=40):
    return pl.pallas_call(
        body,
        out_shape=outs,
        in_specs=ins,
        out_specs=out_specs or [VM] * len(outs),
        scratch_shapes=list(scratch),
        compiler_params=pltpu.CompilerParams(vmem_limit_bytes=limit * 2**20),
        cost_estimate=pl.CostEstimate(flops=int(us * 10**9), bytes_accessed=1000, transcendentals=0),
    )


def dot(x, y):
    return jnp.dot(x, y, preferred_element_type=F32)


def iota(shape, dim):
    return lax.broadcasted_iota(I32, shape, dim)


def zero_one(mask):
    return mask.astype(F32).astype(BF)


def rows_apart(x, atoms):
    block = x.shape[0] // atoms
    size = block // 2
    to, of = iota((block, block), 0), iota((block, block), 1)
    pick = zero_one(of == jnp.where(to < size, 2 * to, 2 * (to - size) + 1))
    wide = jnp.concatenate([x[a * block : (a + 1) * block] for a in range(atoms)], axis=1)
    return dot(pick, wide).astype(BF)


def beside(parts, atoms, span, size):
    rows = []
    for a in range(atoms):
        lanes = [y[p * size : (p + 1) * size, a * span : (a + 1) * span] for p in range(2) for y in parts]
        rows.append(jnp.concatenate(lanes, axis=1))
    return jnp.concatenate(rows, axis=0)


def low_kernel(shifts, weights, x, out, apart, bands):
    atoms, size, span = out.shape
    half = span // 2
    lane = iota((2 * span, span), 1)
    first = lane < half
    gap = iota((2 * span, span), 0) - half - jnp.where(first, lane, lane - half)
    band = jnp.zeros(gap.shape, F32)
    for q in range(shifts.shape[0]):
        band = band + jnp.where(gap == shifts[q], weights[q], 0.0)
    rounded = band.astype(BF).astype(F32)

    def parted(part, mask):
        return jnp.concatenate([jnp.where(mask, part, 0.0), jnp.where(mask, 0.0, part)], axis=0).astype(BF)

    bands[0] = parted(rounded, first)
    bands[1] = parted(band - rounded, first)
    y = rows_apart(x[...], atoms)
    apart[...] = y
    z = beside([y], atoms, span, size)
    cut = slice(half, half + span)
    y = dot(z, parted(rounded[cut], first[cut])) + dot(z, parted((band - rounded)[cut], first[cut]))
    out[...] = y.astype(BF).reshape(out.shape)


def high_kernel(apart, bands, beyond, out):
    atoms, size, span = out.shape
    z = beside([apart[...], rows_apart(beyond[...], atoms)], atoms, span, size)
    y = dot(z, bands[0]) + dot(z, bands[1])
    out[...] = y.astype(BF).reshape(out.shape)


def plan_kernel(names, table, target):
    atoms, nbr = names.shape
    devices = table.shape[0]
    me = lax.axis_index("atom")
    device = iota((devices, nbr), 0)
    ahead = zero_one(iota((nbr, nbr), 0) < iota((nbr, nbr), 1))
    lane = iota(table.shape, 1)
    found = jnp.zeros(table.shape, F32)
    seen = jnp.zeros((devices, 1), F32)
    for a in range(atoms):
        entry = names[a : a + 1, :]
        owner = lax.div(entry, atoms)
        row = entry - owner * atoms
        match = (jnp.broadcast_to(owner, (devices, nbr)) == device).astype(F32)
        rank = dot(match.astype(BF), ahead) + seen
        seen = seen + jnp.sum(match, axis=1, keepdims=True)
        rows = jnp.broadcast_to(row, (devices, nbr)).astype(F32)
        for r in range(CAP):
            here = jnp.where(rank == r, match, 0.0)
            found = found + jnp.where(lane == r, jnp.sum(here * rows, axis=1, keepdims=True), 0.0)
            if a:
                found = found + jnp.where(lane == CAP + r, a * jnp.sum(here, axis=1, keepdims=True), 0.0)
        own_rank = jnp.minimum(jnp.sum(match * rank, axis=0, keepdims=True), CAP - 1.0).astype(I32)
        target[a : a + 1, :] = jnp.where(owner == me, row * atoms + a, atoms * atoms + owner * CAP + own_rank)
    table[...] = found.astype(I32)


def make_first(mates, half):
    def kernel(*refs):
        tables, (low, high, mirror), outs = refs[:mates], refs[mates : mates + 3], refs[mates + 3 :]
        span = low.shape[2]
        me = lax.axis_index("atom")
        for table, out in zip(tables, outs):
            for r in range(CAP):
                row = table[me, r]
                out[r, :, :span] = low[row]
                out[r, :, span : 2 * span] = high[row]
                out[r, :, 2 * span :] = mirror[table[lax.bitwise_xor(me, half), r]]

    return kernel


def make_second(mates, half):
    def kernel(*refs):
        tables, mirror, outs = refs[:mates], refs[mates], refs[mates + 1 :]
        holder = lax.bitwise_xor(lax.axis_index("atom"), half)
        for table, out in zip(tables, outs):
            for r in range(CAP):
                out[r] = mirror[table[holder, r]]

    return kernel


def make_form(orb):
    size = orb * orb
    tail = size - LANES
    reps = LANES // tail
    groups = pl.cdiv(orb, reps)
    height = (orb + groups) * PAD + SKEW

    def kernel(target, x, ops, left, right, sums):
        atoms, nbr = target.shape
        terms = x.shape[0]
        slots = ops.shape[0]
        dirs = terms // (atoms * nbr)
        source, lane = iota((size, LANES), 0), iota((size, LANES), 1)

        def spread(at):
            group = sum(((at >= m * orb).astype(I32) for m in range(1, orb)), jnp.zeros(at.shape, I32))
            return group, at - group * orb

        group, within = spread(lane)
        tail_group, tail_within = spread(LANES + lax.bitwise_and(lane, tail - 1))
        part = lax.shift_right_logical(lane, tail.bit_length() - 1)
        values = x[...]
        left_at, tail_at = source - group, source - part * orb - tail_group
        for i in range(orb):
            left[i] = dot(values, zero_one(left_at == i * orb)).astype(BF)
        for g in range(groups):
            left[orb + g] = dot(values, zero_one(tail_at == g * reps * orb)).astype(BF)
        right_at, tail_right = source - within, source - tail_within
        for f in range(orb):
            right[0, f] = dot(values, zero_one(right_at == f * orb)).astype(BF)
            right[1, f] = dot(values, zero_one(tail_right == f * orb)).astype(BF)
        behind = iota((nbr, terms), 1) - iota((nbr, terms), 0) * dirs
        mask = jnp.zeros((slots, terms), F32)
        for a in range(atoms):
            hit = zero_one(jnp.broadcast_to(target[a : a + 1, :], (slots, nbr)) == iota((slots, nbr), 0))
            shifted = behind - a * nbr * dirs
            mask = mask + dot(hit, zero_one((shifted >= 0) & (shifted < dirs)))
        mask = mask.astype(BF)
        for i in range(orb + groups):
            c = i // orb
            lhs = left[i]
            for f in range(0, orb, 2):
                pair = [lhs * right[c, f + m] for m in range(2)]
                found = dot(mask, jnp.concatenate(pair, axis=1))
                for m in range(2):
                    sums[pl.ds(i * PAD + f + m, slots, stride=height), :] = found[:, m * LANES : (m + 1) * LANES]
        at = lax.shift_right_logical(iota((PAD, LANES), 1), tail.bit_length() - 1)
        only = [zero_one(at == m) for m in range(reps)]

        def settle(slot, carry):
            base = slot * height

            def tile(i):
                return sums[pl.ds(pl.multiple_of(base + i * PAD, PAD), PAD), :].astype(BF)

            packed = [tile(orb + g) for g in range(groups)]
            for i in range(orb):
                ops[slot, i * PAD : (i + 1) * PAD, :LANES] = tile(i)
                ops[slot, i * PAD : (i + 1) * PAD, LANES:] = packed[i // reps] * only[i % reps]
            return carry

        lax.fori_loop(0, slots, settle, 0, unroll=4)

    return kernel


def tall(block):
    tail = block.shape[0] - LANES
    return jnp.concatenate([block[:LANES]] + [block[LANES:]] * (LANES // tail), axis=0)


def make_local(mates, half):
    def kernel(*refs):
        table, ops = refs[:2]
        own, mirror = refs[2:4], refs[4:6]
        near, total = refs[6 : 6 + mates], refs[-1]
        atoms, height, wide = total.shape
        me = lax.axis_index("atom")
        run = jnp.zeros((atoms * height, wide), F32)
        for b in range(atoms):
            block = tall(jnp.concatenate([own[0][b], own[1][b]], axis=1))
            lhs = ops[b * atoms : (b + 1) * atoms].reshape(atoms * height, ops.shape[2])
            run = run + dot(lhs, block)
        total[...] = run.reshape(total.shape)
        for s in range(mates):
            for r in range(CAP):
                owner = lax.bitwise_xor(me, mates - s)
                total[table[owner, CAP + r]] += dot(ops[atoms * atoms + owner * CAP + r], tall(near[s][r, :, :wide]))
        for r in range(CAP):
            owner = lax.bitwise_xor(me, half)
            row = table[owner, r]
            block = tall(jnp.concatenate([mirror[0][row], mirror[1][row]], axis=1))
            total[table[owner, CAP + r]] += dot(ops[atoms * atoms + owner * CAP + r], block)

    return kernel


def make_final(mates, half, orb):
    size = orb * orb

    def kernel(*refs):
        table, ops, begun = refs[:3]
        first, second = refs[3 : 3 + mates], refs[3 + mates : 3 + 2 * mates]
        out, total = refs[-2:]
        atoms, height, wide = total.shape
        span = wide // 2
        part = span // 2
        me = lax.axis_index("atom")
        total[...] = begun[...]
        for s in range(mates):
            for r in range(CAP):
                owner = lax.bitwise_xor(me, half + mates - s)
                block = tall(jnp.concatenate([first[s][r, :, wide:], second[s][r]], axis=1))
                total[table[owner, CAP + r]] += dot(ops[atoms * atoms + owner * CAP + r], block)

        to, of = iota((2 * size, height), 0), iota((2 * size, height), 1)
        f = lax.bitwise_and(of, PAD - 1)
        at = 2 * (lax.shift_right_logical(of, PAD.bit_length() - 1) * orb + f)
        even = zero_one((to == at) & (f < orb))
        odd = zero_one((to == at + 1) & (f < orb))
        real = lax.bitwise_and(iota((height, span), 0), PAD - 1) < orb
        parts = [[], []]
        for a in range(atoms):
            for p in range(2):
                lanes = [total[a, :, h * span + p * part : h * span + (p + 1) * part] for h in range(2)]
                parts[p].append(jnp.where(real, jnp.concatenate(lanes, axis=1), 0.0).astype(BF))
        rows = dot(even, jnp.concatenate(parts[0], axis=1)) + dot(odd, jnp.concatenate(parts[1], axis=1))
        for a in range(atoms):
            out[a * 2 * size : (a + 1) * 2 * size, :] = rows[:, a * span : (a + 1) * span].astype(BF)

    return kernel


def after(value, *earlier):
    return lax.optimization_barrier((value,) + earlier)[0]


def on_device(green, coupling, neighbours, shifts, weights):
    atoms, _, orb, _, span = green.shape
    size = orb * orb
    devices = lax.axis_size("atom")
    half = devices // 2
    mates = half - 1
    peers = lax.axis_size("energy")
    shape = jax.ShapeDtypeStruct

    def across(value, by):
        return lax.ppermute(value, "atom", [(i, i ^ by) for i in range(devices)])

    x = green.transpose(0, 2, 3, 1, 4).reshape(atoms * size * 2, span)
    unit = shape((atoms, size, span), BF)
    low, apart, bands = call(
        low_kernel,
        [unit, shape((2 * size, atoms * span), BF), shape((2, 4 * span, span), BF)],
        [SM, SM, VM],
        us=0.01,
    )(shifts, weights, x)
    beyond = lax.ppermute(after(x, low), "energy", [(i, i - 1) for i in range(1, peers)])
    (high,) = call(high_kernel, [unit], [VM] * 3, us=0.7)(apart, bands, beyond)
    mirror = across(low, half), across(high, half)
    table, target = call(plan_kernel, [shape((devices, LANES), I32), shape(neighbours.shape, I32)], [VM], us=0.5)(
        neighbours
    )
    tables = [across(after(table, high), s) for s in reversed(range(1, half))]
    triple, single = shape((CAP, size, 3 * span), BF), shape((CAP, size, span), BF)
    first_out = call(make_first(mates, half), [triple] * mates, [SM] * mates + [VM] * 3)(*tables, low, high, mirror[0])
    near = [across(v, mates - s) for s, v in enumerate(first_out)]
    second_out = call(make_second(mates, half), [single] * mates, [SM] * mates + [VM])(*tables, mirror[1])
    far = [across(v, mates - s) for s, v in enumerate(second_out)]

    terms = coupling.reshape(-1, size)
    height, groups = orb * PAD, pl.cdiv(orb, LANES // (size - LANES))
    slots = atoms * atoms + devices * CAP
    (ops,) = call(
        make_form(orb),
        [shape((slots, height, 2 * LANES), BF)],
        [VM, VM],
        None,
        [
            pltpu.VMEM((orb + groups, terms.shape[0], LANES), BF),
            pltpu.VMEM((2, orb, terms.shape[0], LANES), BF),
            pltpu.VMEM(((slots + 1) * (height + groups * PAD + SKEW), LANES), F32),
        ],
        us=0.01,
    )(target, terms)

    total = shape((atoms, height, 2 * span), F32)
    (begun,) = call(make_local(mates, half), [total], [SM] + [VM] * (5 + mates), us=1.5)(
        table, ops, low, high, *mirror, *near
    )
    (out,) = call(
        make_final(mates, half, orb),
        [shape(x.shape, BF)],
        [SM] + [VM] * (2 + 2 * mates),
        None,
        [pltpu.VMEM(total.shape, F32)],
    )(table, ops, begun, *near, *far)
    return out.reshape(atoms, orb, orb, 2, span).transpose(0, 3, 1, 2, 4)


def solution(mesh):
    placed = (P("atom", None, None, None, "energy"), P("atom", None), P("atom", None), P(), P())
    return jax.shard_map(
        on_device,
        mesh=mesh,
        in_specs=placed,
        out_specs=P("atom", None, None, None, "energy"),
        check_vma=False,
    )
```
